512 devices in a mesh: dp: 16 (over x, z_lo), centre: 32 (over y, z_hi, core).
Axes of the slice: x: 4, y: 8, z: 8 (z_hi: 2, z_lo: 4; z = z_hi * 4 + z_lo), core: 2. Of those that a mesh axis runs over, the one named last changes fastest.
Arguments:
- samples: bfloat16 [524288, 256], P(('dp', 'centre')), may hold values from -9 to 9
- centres: bfloat16 [4096, 256], P('centre'), may hold values from -6 to 6
- factor: float32 [4096, 4096], P('centre'), as said below
- solution: float32 [4096], P('centre'), may hold values from -6 to 6
- residual: float32 [4096], P('centre'), may hold values from -6 to 6
- direction: float32 [4096], P('centre'), may hold values from -6 to 6
Outputs:
- new_solution: float32 [4096], P('centre')
- new_residual: float32 [4096], P('centre')
- new_direction: float32 [4096], P('centre')
The draws below stay inside these ranges and needn't reach their ends.
Inputs may be any that keep to these rules, and one draw needn't show every extreme that they name: factor is upper triangular with a positive diagonal.
All inputs are finite; a program needn't handle non-finite values.
Results may differ from the reference program's by a relative error of at most 0.002.
Values may be sent and summed in bfloat16 or wider, within the bound.
A program may use at most 64 MiB of HBM per device.

```python
import math
import jax
import jax.numpy as jnp
from jax import lax

D = 256
SAMP_DEV = 1024
SAMPLES = 524288
M = 4096


def centre_rows(key):
    return jnp.clip(jax.random.normal(key, (M, D), jnp.float32), -6.0, 6.0)


def mixed_rows(key, shared, spread, noise):
    owner_key, mix_key = jax.random.split(key)
    owners = jax.random.randint(owner_key, (SAMPLES,), 0, M)
    middle = (math.log(4.0) + 1.5 * math.log(M)) / 24.0
    mixing = jax.random.uniform(mix_key, (SAMPLES, 1), jnp.float32, middle - spread, middle + spread)
    return mixing * shared[owners] + jnp.sqrt(1.0 - mixing * mixing) * noise


def draw_centres(key, part):
    shared = centre_rows(key)
    return shared.astype(jnp.bfloat16)


def draw_samples(key, part):
    shared = centre_rows(key)
    key = jax.random.fold_in(key, 11)
    base_key, noise_key = jax.random.split(key)
    noise = jnp.clip(jax.random.normal(noise_key, (SAMPLES, D), jnp.float32), -6.0, 6.0)
    rows = mixed_rows(base_key, shared, 0.1, noise)
    return rows.astype(jnp.bfloat16)


def draw_factor(key, part):
    key = jax.random.fold_in(key, 7)
    first_key, second_key = jax.random.split(key)
    row_ids = jnp.arange(M)[:, None]
    col_ids = jnp.arange(M)[None, :]
    diagonal = jnp.exp(jax.random.uniform(first_key, (M, M), jnp.float32, math.log(0.5), math.log(2.0)))
    offdiag = jax.random.normal(second_key, (M, M), jnp.float32) * 0.3
    offdiag = offdiag / math.sqrt(M)
    return jnp.where(col_ids == row_ids, diagonal, jnp.where(col_ids > row_ids, offdiag, 0.0)).astype(jnp.float32)


def block_levels(own_key, shape, shards, smallest, high):
    gain = 1.0
    for dim, blocks in shards:
        steps = jax.random.uniform(jax.random.fold_in(jax.random.fold_in(own_key, 6), dim), (blocks,), jnp.float32, smallest / len(shards), high / len(shards))
        gain = gain * jnp.repeat(jnp.exp(steps), shape[dim] // blocks).reshape((-1,) + (1,) * (len(shape) - 1 - dim))
    return gain


def gaussian(key, shape, scale, limit, cuts=(), held_as=jnp.bfloat16):
    array = jax.random.normal(key, shape, jnp.float32) * scale
    if len(cuts) > 0:
        array = block_levels(key, shape, cuts, -0.22, 0.18) * array
    return jnp.clip(array, min=-limit, max=limit).astype(held_as)


def setup_inputs(seed: int = 0) -> dict:
    arg_keys = jax.random.split(jax.random.key(seed), 7)
    samples = draw_samples(jax.random.fold_in(arg_keys[6], 71), 0)
    centres = draw_centres(jax.random.fold_in(arg_keys[6], 71), 0)
    factor = draw_factor(jax.random.fold_in(arg_keys[6], 71), 0)
    solution = gaussian(arg_keys[3], (M,), 1.0, 6.0, ((0, 32),), jnp.float32)
    residual = gaussian(arg_keys[4], (M,), 1.0, 6.0, ((0, 32),), jnp.float32)
    direction = gaussian(arg_keys[5], (M,), 1.0, 6.0, ((0, 32),), jnp.float32)
    return {"samples": samples, "centres": centres, "factor": factor, "solution": solution, "residual": residual, "direction": direction}


sharpness = 6.0
ridge = 0.3
balance = 16.0

def reference(samples, centres, factor, solution, residual, direction):
    mapped = jnp.dot(factor, direction, precision=lax.Precision.HIGHEST).astype(jnp.bfloat16)
    col_norms = lax.optimization_barrier(jnp.sum(jnp.square(centres.astype(jnp.float32)), axis=1))
    blocks = samples.reshape(-1, SAMP_DEV, D)

    def one_block(total, rows):
        row_norms = lax.optimization_barrier(jnp.sum(jnp.square(rows.astype(jnp.float32)), axis=1))
        cross = jnp.dot(rows, centres.T, preferred_element_type=jnp.float32)
        dist = row_norms[:, None] + col_norms[None, :] - 2.0 * cross
        tile = jnp.exp(sharpness * (2.0 - dist / D)).astype(jnp.bfloat16)
        weights = jnp.dot(tile, mapped, preferred_element_type=jnp.float32).astype(jnp.bfloat16)
        return (total + jnp.dot(weights, tile, preferred_element_type=jnp.float32), None)
    columns, unused = lax.scan(one_block, jnp.zeros((M,), jnp.float32), blocks)
    image = jnp.dot(columns, factor, precision=lax.Precision.HIGHEST) / (balance * SAMPLES * math.sqrt(M)) + ridge * direction
    old_norm = jnp.sum(residual * residual)
    alpha = old_norm / jnp.sum(direction * image)
    new_solution = solution + alpha * direction
    new_residual = residual - alpha * image
    new_norm = jnp.sum(new_residual * new_residual)
    new_direction = new_residual + new_norm / old_norm * direction
    return (new_solution, new_residual, new_direction)
```

```python
import functools
import math

import jax
import jax.numpy as jnp
from jax import lax
from jax.experimental import pallas as pl
from jax.experimental.pallas import tpu as pltpu
from jax.sharding import PartitionSpec as P

sharpness = 6.0
ridge = 0.3
balance = 16.0
MESH = pl.DeviceIdType.MESH
F32 = jnp.float32
BF16 = jnp.bfloat16


def step_kernel(
    n_dp,
    n_ce,
    scale,
    samples_hbm,
    centres_hbm,
    factor_hbm,
    sol_ref,
    res_ref,
    dir_ref,
    new_sol_ref,
    new_res_ref,
    new_dir_ref,
    smp,
    cen,
    fac,
    tiles,
    row_term,
    a_buf,
    m_buf,
    c_out,
    c_buf,
    g_buf,
    i_out,
    i_buf,
    e_buf,
    load_sem,
    cen_recv,
    cen_send,
    small_recv,
    small_send,
):
    dp = lax.axis_index("dp")
    me = lax.axis_index("centre")
    rows, depth = cen.shape[1], cen.shape[2]
    width = smp.shape[0]
    n_y = n_ce // 4
    n_tiles = n_ce // 2

    load_cen = pltpu.make_async_copy(centres_hbm, cen.at[me], load_sem.at[0])
    load_smp = pltpu.make_async_copy(samples_hbm, smp, load_sem.at[1])
    load_fac = pltpu.make_async_copy(factor_hbm, fac, load_sem.at[2])
    load_cen.start()
    load_smp.start()
    load_fac.start()

    barrier = pltpu.get_barrier_semaphore()

    @pl.loop(1, n_ce)
    def _(k):
        peer = lax.rem(me + k, n_ce)
        pl.semaphore_signal(barrier, inc=1, device_id=(dp, peer), device_id_type=MESH)

    @pl.loop(1, n_dp)
    def _(k):
        peer = lax.rem(dp + k, n_dp)
        pl.semaphore_signal(barrier, inc=1, device_id=(peer, me), device_id_type=MESH)

    residual = res_ref[...]
    direction = dir_ref[...]
    a_buf[me, :, 0:rows] = direction
    a_buf[me, :, rows : 2 * rows] = residual * residual
    pl.semaphore_wait(barrier, n_ce + n_dp - 2)

    def push_all(phase, source, landing):
        @pl.loop(1, n_ce)
        def _(k):
            peer = lax.rem(me + k, n_ce)
            pltpu.make_async_remote_copy(
                src_ref=source(peer),
                dst_ref=landing.at[me],
                send_sem=small_send.at[phase],
                recv_sem=small_recv.at[phase],
                device_id=(dp, peer),
                device_id_type=MESH,
            ).start()

    def wait_all(phase, landing, sems):
        part = landing.at[pl.ds(0, landing.shape[0] - 1)]
        pltpu.make_async_copy(part, part, sems.at[phase]).wait()

    def send_cen(slot, peer):
        pltpu.make_async_remote_copy(
            src_ref=cen.at[slot],
            dst_ref=cen.at[slot],
            send_sem=cen_send,
            recv_sem=cen_recv.at[slot],
            device_id=(dp, peer),
            device_id_type=MESH,
        ).start()

    def wait_cen(slot):
        pltpu.make_async_copy(cen.at[slot], cen.at[slot], cen_recv.at[slot]).wait()

    up = lax.rem(me + 4, n_ce)
    down = lax.rem(me + n_ce - 4, n_ce)
    core = lax.rem(me, 2)
    sibling = me + 1 - 2 * core
    half = lax.rem(me // 2, 2)
    across = me + 2 - 4 * half

    push_all(0, lambda peer: a_buf.at[me], a_buf)
    load_cen.wait()
    send_cen(me, up)
    send_cen(me, down)
    send_cen(me, across)
    send_cen(me, sibling)

    log2e = math.log2(math.e)
    unit = sharpness / depth * log2e

    load_smp.wait()
    for part in range(width // rows):
        block = smp[part * rows : (part + 1) * rows, :].astype(F32)
        square = block * block
        folded = square[:, 0:rows]
        for other in range(1, depth // rows):
            folded = folded + square[:, other * rows : (other + 1) * rows]
        norms = jnp.sum(folded.T, axis=0, keepdims=True)
        row_term[:, part * rows : (part + 1) * rows] = (2.0 * sharpness * log2e) - unit * norms

    def make_tile(tile):
        block = cen[pl.ds(2 * tile, 2)].reshape(2 * rows, depth)
        wide = block.astype(F32)
        norms = jnp.sum(wide * wide, axis=1, keepdims=True) * unit
        cross = lax.dot_general(
            block, smp[...], (((1,), (1,)), ((), ())), preferred_element_type=F32
        )
        power = cross * (2.0 * unit) + (row_term[...] - norms)
        tiles[tile] = jnp.exp2(power).astype(BF16)

    wait_cen(sibling)
    make_tile(me // 2)

    load_fac.wait()
    wait_all(0, a_buf, small_recv)
    acc = fac[:, 0:rows] * a_buf[0, :, 0:rows]
    for b in range(1, n_ce):
        acc = acc + fac[:, b * rows : (b + 1) * rows] * a_buf[b, :, 0:rows]
    m_buf[me] = jnp.sum(acc.T, axis=0, keepdims=True)
    push_all(1, lambda peer: m_buf.at[me], m_buf)

    wait_cen(across)
    send_cen(across, up)
    send_cen(across, down)
    send_cen(across, sibling)
    wait_cen(across + 1 - 2 * core)
    make_tile(across // 2)

    @pl.loop(1, n_y // 2)
    def _(s):
        for first in (me, across):
            low = lax.rem(first + n_ce - 4 * s, n_ce)
            high = lax.rem(first + 4 * s, n_ce)
            wait_cen(low)
            send_cen(low, up)
            send_cen(low, sibling)
            wait_cen(high)

            @pl.when(s < n_y // 2 - 1)
            def _():
                send_cen(high, down)

            send_cen(high, sibling)
            wait_cen(low + 1 - 2 * core)
            make_tile(low // 2)
            wait_cen(high + 1 - 2 * core)
            make_tile(high // 2)

    for first in (me, across):
        far = lax.rem(first + n_ce // 2, n_ce)
        wait_cen(far)
        send_cen(far, sibling)
        wait_cen(far + 1 - 2 * core)
        make_tile(far // 2)

    wait_all(1, m_buf, small_recv)

    def add_weights(tile, total):
        coeffs = jnp.concatenate([m_buf[2 * tile], m_buf[2 * tile + 1]], axis=1)
        coeffs = jnp.broadcast_to(coeffs, (16, 2 * rows)).astype(BF16)
        return total + jnp.dot(coeffs, tiles[tile], preferred_element_type=F32)

    weights = lax.fori_loop(0, n_tiles, add_weights, jnp.zeros((16, width), F32)).astype(BF16)

    @pl.loop(0, n_tiles)
    def _(tile):
        part = lax.dot_general(
            weights, tiles[tile], (((1,), (1,)), ((), ())), preferred_element_type=F32
        )
        c_out[2 * tile] = part[0:1, 0:rows]
        c_out[2 * tile + 1] = part[0:1, rows : 2 * rows]

    c_buf[me] = c_out[me]
    push_all(2, lambda peer: c_out.at[peer], c_buf)
    wait_all(2, c_buf, small_recv)
    g_buf[dp] = jnp.sum(c_buf[...], axis=0)

    @pl.loop(1, n_dp)
    def _(k):
        peer = lax.rem(dp + k, n_dp)
        pltpu.make_async_remote_copy(
            src_ref=g_buf.at[dp],
            dst_ref=g_buf.at[dp],
            send_sem=small_send.at[3],
            recv_sem=small_recv.at[3],
            device_id=(peer, me),
            device_id_type=MESH,
        ).start()

    wait_all(3, g_buf, small_recv)
    columns = jnp.sum(g_buf[...], axis=0) * scale

    spread = jnp.broadcast_to(columns, (rows, rows)).T
    bend = m_buf[me] * columns
    for b in range(n_ce):
        i_out[b, :, 0:rows] = jnp.sum(
            fac[:, b * rows : (b + 1) * rows] * spread, axis=0, keepdims=True
        )
        i_out[b, :, rows : 2 * rows] = bend
    i_buf[me] = i_out[me]
    push_all(4, lambda peer: i_out.at[peer], i_buf)
    gathered = jnp.sum(a_buf[:, :, rows : 2 * rows], axis=0)
    old_norm = jnp.sum(gathered, axis=1, keepdims=True)
    whole = a_buf[:, :, 0:rows]
    dir_norm = jnp.sum(jnp.sum(whole * whole, axis=0), axis=1, keepdims=True)
    wait_all(4, i_buf, small_recv)
    both = jnp.sum(i_buf[...], axis=0)
    image = both[:, 0:rows] + ridge * direction
    curvature = jnp.sum(both[:, rows : 2 * rows], axis=1, keepdims=True) + ridge * dir_norm
    alpha = old_norm / curvature
    new_residual = residual - alpha * image
    e_buf[me] = new_residual * new_residual
    push_all(5, lambda peer: e_buf.at[me], e_buf)
    new_sol_ref[...] = sol_ref[...] + alpha * direction
    new_res_ref[...] = new_residual
    wait_all(5, e_buf, small_recv)
    new_norm = jnp.sum(jnp.sum(e_buf[...], axis=0), axis=1, keepdims=True)
    new_dir_ref[...] = new_residual + new_norm / old_norm * direction

    for phase, landing in ((0, a_buf), (1, m_buf), (2, c_buf), (3, g_buf), (4, i_buf), (5, e_buf)):
        wait_all(phase, landing, small_send)
    sent = cen.at[pl.ds(0, n_ce - 1)]
    pltpu.make_async_copy(sent, sent, cen_send).wait()


def on_device(n_dp, n_ce, samples, centres, factor, solution, residual, direction):
    rows, depth = centres.shape
    width = samples.shape[0]
    total_samples = width * n_dp * n_ce
    scale = 1.0 / (balance * total_samples * math.sqrt(rows * n_ce))
    vector = jax.ShapeDtypeStruct((1, rows), F32)
    vmem = pl.BlockSpec(memory_space=pltpu.VMEM)
    anywhere = pl.BlockSpec(memory_space=pl.ANY)
    outs = pl.pallas_call(
        functools.partial(step_kernel, n_dp, n_ce, scale),
        out_shape=(vector, vector, vector),
        in_specs=[anywhere, anywhere, anywhere, vmem, vmem, vmem],
        out_specs=(vmem, vmem, vmem),
        scratch_shapes=[
            pltpu.VMEM((width, depth), BF16),
            pltpu.VMEM((n_ce, rows, depth), BF16),
            pltpu.VMEM((rows, rows * n_ce), F32),
            pltpu.VMEM((n_ce // 2, 2 * rows, width), BF16),
            pltpu.VMEM((1, width), F32),
            pltpu.VMEM((n_ce, 1, 2 * rows), F32),
            pltpu.VMEM((n_ce, 1, rows), F32),
            pltpu.VMEM((n_ce, 1, rows), F32),
            pltpu.VMEM((n_ce, 1, rows), F32),
            pltpu.VMEM((n_dp, 1, rows), F32),
            pltpu.VMEM((n_ce, 1, 2 * rows), F32),
            pltpu.VMEM((n_ce, 1, 2 * rows), F32),
            pltpu.VMEM((n_ce, 1, rows), F32),
            pltpu.SemaphoreType.DMA((3,)),
            pltpu.SemaphoreType.DMA((n_ce,)),
            pltpu.SemaphoreType.DMA,
            pltpu.SemaphoreType.DMA((6,)),
            pltpu.SemaphoreType.DMA((6,)),
        ],
        compiler_params=pltpu.CompilerParams(
            collective_id=0, has_side_effects=True, vmem_limit_bytes=40 * 1024 * 1024
        ),
        cost_estimate=pl.CostEstimate(
            flops=2 * width * rows * n_ce * (depth + 2),
            bytes_accessed=4 * rows * rows * n_ce,
            transcendentals=width * rows * n_ce,
        ),
    )(
        samples,
        centres,
        factor,
        solution.reshape(1, rows),
        residual.reshape(1, rows),
        direction.reshape(1, rows),
    )
    return tuple(out.reshape(rows) for out in outs)


def solution(mesh):
    return jax.shard_map(
        functools.partial(on_device, mesh.shape["dp"], mesh.shape["centre"]),
        mesh=mesh,
        in_specs=(
            P(("dp", "centre"), None),
            P("centre", None),
            P("centre", None),
            P("centre"),
            P("centre"),
            P("centre"),
        ),
        out_specs=(P("centre"), P("centre"), P("centre")),
        check_vma=False,
    )
```

```python
import functools
import math

import jax
import jax.numpy as jnp
from jax import lax
from jax.experimental import pallas as pl
from jax.experimental.pallas import tpu as pltpu
from jax.sharding import PartitionSpec as P

sharpness = 6.0
ridge = 0.3
balance = 16.0
z_low = 4
MESH = pl.DeviceIdType.MESH
F32 = jnp.float32
BF16 = jnp.bfloat16


def step_kernel(
    n_dp,
    n_ce,
    scale,
    samples_hbm,
    centres_hbm,
    factor_hbm,
    res_hbm,
    dir_hbm,
    out_ref,
    smp,
    cen,
    fac,
    res_ref,
    dir_ref,
    tiles,
    row_term,
    a_buf,
    m_buf,
    c_out,
    c_buf,
    g_out,
    g_buf,
    i_out,
    i_buf,
    e_buf,
    left_ref,
    load_sem,
    cen_recv,
    cen_send,
    small_recv,
    small_send,
    token,
):
    dp = lax.axis_index("dp")
    me = lax.axis_index("centre")
    rows, depth = cen.shape[1], cen.shape[2]
    width = smp.shape[0]
    n_y = n_ce // 4
    n_q = 2 * n_y
    n_x = n_dp // z_low
    n_z = 2 * z_low
    n_p = n_x * n_z
    n_tiles = n_ce // 2
    x, low_z = dp // z_low, lax.rem(dp, z_low)
    y, half, core = me // 4, lax.rem(me // 2, 2), lax.rem(me, 2)
    z = half * z_low + low_z
    mine = y * 2 + core
    place = x * n_z + z

    def column_peer(k):
        q = lax.rem(mine + k, n_q)
        return q, (dp, (q // 2) * 4 + half * 2 + lax.rem(q, 2))

    def z_peer(k):
        other = lax.rem(z + k, n_z)
        return (x * z_low + lax.rem(other, z_low), y * 4 + (other // z_low) * 2 + core)

    def plane_peer(k):
        p = lax.rem(place + k, n_p)
        other = lax.rem(p, n_z)
        there = (p // n_z) * z_low + lax.rem(other, z_low)
        return other // z_low, (there, y * 4 + (other // z_low) * 2 + core)

    def group_peer(k):
        peer = lax.rem(me + k, n_ce)
        return (peer // 4) * 2 + lax.rem(peer, 2), (dp, peer)

    up = lax.rem(me + 4, n_ce)
    down = lax.rem(me + n_ce - 4, n_ce)
    sibling = me + 1 - 2 * core
    across = me + 2 - 4 * half

    loads = [
        pltpu.make_async_copy(dir_hbm, dir_ref, load_sem.at[0]),
        pltpu.make_async_copy(res_hbm, res_ref, load_sem.at[1]),
        pltpu.make_async_copy(centres_hbm, cen.at[me], load_sem.at[2]),
        pltpu.make_async_copy(samples_hbm, smp, load_sem.at[3]),
        pltpu.make_async_copy(factor_hbm, fac, load_sem.at[4]),
    ]
    for load in loads:
        load.start()

    barrier = pltpu.get_barrier_semaphore()

    @pl.loop(1, n_q)
    def _(k):
        pl.semaphore_signal(barrier, inc=1, device_id=column_peer(k)[1], device_id_type=MESH)

    @pl.loop(1, n_z)
    def _(k):
        pl.semaphore_signal(barrier, inc=1, device_id=z_peer(k), device_id_type=MESH)

    @pl.loop(1, n_x)
    def _(k):
        peer = lax.rem(x + k, n_x) * z_low + low_z
        pl.semaphore_signal(barrier, inc=1, device_id=(peer, me), device_id_type=MESH)

    def copy_small(source, target, slot, device):
        pltpu.make_async_remote_copy(
            src_ref=source,
            dst_ref=target,
            send_sem=small_send.at[slot],
            recv_sem=small_recv.at[slot],
            device_id=device,
            device_id_type=MESH,
        ).start()

    def wait_small(landing, count, slot, sems):
        part = landing.at[pl.ds(0, count)]
        pltpu.make_async_copy(part, part, sems.at[slot]).wait()

    def send_cen(slot, peer, part=slice(None), sem=None):
        pltpu.make_async_remote_copy(
            src_ref=cen.at[slot, part],
            dst_ref=cen.at[slot, part],
            send_sem=cen_send,
            recv_sem=cen_recv.at[slot if sem is None else sem],
            device_id=(dp, peer),
            device_id_type=MESH,
        ).start()

    def wait_cen(slot, part=slice(None), sem=None):
        landed = cen.at[slot, part]
        pltpu.make_async_copy(
            landed, landed, cen_recv.at[slot if sem is None else sem]
        ).wait()

    loads[0].wait()
    loads[1].wait()
    a_buf[me, :, 0:rows] = dir_ref[...]
    a_buf[me, :, rows : 2 * rows] = res_ref[...]
    loads[2].wait()

    log2e = math.log2(math.e)
    unit = sharpness / depth * log2e
    loads[3].wait()
    for part in range(width // rows):
        block = smp[part * rows : (part + 1) * rows, :].astype(F32)
        square = block * block
        folded = square[:, 0:rows]
        for other in range(1, depth // rows):
            folded = folded + square[:, other * rows : (other + 1) * rows]
        norms = jnp.sum(folded.T, axis=0, keepdims=True)
        row_term[:, part * rows : (part + 1) * rows] = (2.0 * sharpness * log2e) - unit * norms

    pl.semaphore_wait(barrier, n_q + n_z + n_x - 3)

    copy_small(a_buf.at[me], a_buf.at[me], 1, (dp, across))

    @pl.loop(1, n_q)
    def _(k):
        copy_small(a_buf.at[me], a_buf.at[me], 0, column_peer(k)[1])

    send_cen(me, across)
    send_cen(me, up)
    send_cen(me, down)
    send_cen(me, sibling)

    @pl.loop(1, n_z)
    def _(k):
        pl.semaphore_signal(token, inc=1, device_id=z_peer(k), device_id_type=MESH)

    def make_tile(slot):
        tile = slot // 2
        block = cen[pl.ds(2 * tile, 2)].reshape(2 * rows, depth)
        wide = block.astype(F32)
        norms = jnp.sum(wide * wide, axis=1, keepdims=True) * unit
        cross = lax.dot_general(
            block, smp[...], (((1,), (1,)), ((), ())), preferred_element_type=F32
        )
        power = cross * (2.0 * unit) + (row_term[...] - norms)
        tiles[tile] = jnp.exp2(power).astype(BF16)

    def twin(slot):
        return slot + 1 - 2 * core

    def pull(first, s):
        low = lax.rem(first + n_ce - 4 * s, n_ce)
        high = lax.rem(first + 4 * s, n_ce)
        wait_cen(low)
        if s < n_y // 2 - 1:
            send_cen(low, up)
        else:
            send_cen(low, up, top)
        send_cen(low, sibling)
        wait_cen(high)
        if s < n_y // 2 - 1:
            send_cen(high, down)
        else:
            send_cen(high, down, bottom, n_ce + far_sem[first is across])
        send_cen(high, sibling)
        return [low, high]

    def pull_far(first):
        far = lax.rem(first + n_ce // 2, n_ce)
        wait_cen(far, top)
        wait_cen(far, bottom, n_ce + far_sem[first is across])
        send_cen(far, sibling)
        return [far]

    top, bottom = slice(0, rows // 2), slice(rows // 2, rows)
    far_sem = {False: 0, True: 1}

    def work(slots):
        for slot in slots:
            wait_cen(twin(slot))
            make_tile(slot)

    work([me])
    wait_small(a_buf, 1, 1, small_recv)

    @pl.loop(1, n_q)
    def _(k):
        copy_small(a_buf.at[across], a_buf.at[across], 2, column_peer(k)[1])

    near = pull(me, 1)
    wait_cen(across)
    send_cen(across, up)
    send_cen(across, down)
    send_cen(across, sibling)
    work(near)
    next_own = pull(me, 2)
    work([across])
    next_far = pull(across, 1)
    work(next_own)

    wait_small(a_buf, n_q - 1, 0, small_recv)
    wait_small(a_buf, n_q - 1, 2, small_recv)
    loads[4].wait()
    acc = fac[:, 0:rows] * a_buf[0, :, 0:rows]
    for b in range(1, n_ce):
        acc = acc + fac[:, b * rows : (b + 1) * rows] * a_buf[b, :, 0:rows]
    m_buf[me] = jnp.sum(acc.T, axis=0, keepdims=True)

    @pl.loop(1, n_ce)
    def _(k):
        copy_small(m_buf.at[me], m_buf.at[me], 3, group_peer(k)[1])

    next_own = pull(me, 3)
    work(next_far)
    next_far = pull(across, 2)
    work(next_own)
    next_own = pull_far(me)
    work(next_far)
    next_far = pull(across, 3)
    work(next_own)
    work(next_far)
    work(pull_far(across))

    wait_small(m_buf, n_ce - 1, 3, small_recv)

    def add_weights(tile, total):
        coeffs = jnp.concatenate([m_buf[2 * tile], m_buf[2 * tile + 1]], axis=1)
        coeffs = jnp.broadcast_to(coeffs, (16, 2 * rows)).astype(BF16)
        return total + jnp.dot(coeffs, tiles[tile], preferred_element_type=F32)

    weights = lax.fori_loop(0, n_tiles, add_weights, jnp.zeros((16, width), F32))
    upright = jnp.broadcast_to(weights[0:1], (rows, width)).T.astype(BF16)
    diagonal = lax.broadcasted_iota(jnp.int32, (rows, rows), 0) == lax.broadcasted_iota(
        jnp.int32, (rows, rows), 1
    )

    @pl.loop(0, n_y)
    def _(row):
        for side in range(2):
            part = jnp.dot(tiles[2 * row + side], upright, preferred_element_type=F32)
            for c in range(2):
                picked = jnp.where(diagonal, part[c * rows : (c + 1) * rows], 0.0)
                c_out[2 * row + c, :, side * rows : (side + 1) * rows] = jnp.sum(
                    picked, axis=0, keepdims=True
                )

    c_buf[mine] = c_out[mine]

    @pl.loop(1, n_q)
    def _(k):
        q, device = column_peer(k)
        copy_small(c_out.at[q], c_buf.at[mine], 4, device)

    wait_small(c_buf, n_q - 1, 4, small_recv)
    both = jnp.sum(c_buf[...], axis=0)
    g_out[0] = both[:, 0:rows]
    g_out[1] = both[:, rows : 2 * rows]
    pl.semaphore_wait(token, n_z - 1)

    @pl.loop(1, n_p)
    def _(k):
        side, device = plane_peer(k)
        copy_small(g_out.at[side], g_buf.at[place], 5, device)

    g_buf[place] = g_out[half]
    wait_small(g_buf, n_p - 1, 5, small_recv)
    columns = jnp.sum(g_buf[...], axis=0) * scale

    spread = jnp.broadcast_to(columns, (rows, rows)).T
    bend = m_buf[me] * columns
    for b in range(n_ce):
        q, side = (b // 4) * 2 + b % 2, (b // 2) % 2
        i_out[q, :, side * rows : (side + 1) * rows] = jnp.sum(
            fac[:, b * rows : (b + 1) * rows] * spread, axis=0, keepdims=True
        )
        if side == 0:
            i_out[q, :, 2 * rows : 3 * rows] = bend

    @pl.loop(1, n_ce)
    def _(k):
        q, device = group_peer(k)
        copy_small(i_out.at[q], i_buf.at[me], 6, device)

    i_buf[me] = i_out[mine]
    whole_dir = a_buf[:, :, 0:rows]
    whole_res = a_buf[:, :, rows : 2 * rows]
    dir_norm = jnp.sum(jnp.sum(whole_dir * whole_dir, axis=0), axis=1, keepdims=True)
    old_norm = jnp.sum(jnp.sum(whole_res * whole_res, axis=0), axis=1, keepdims=True)
    pair = me - 2 * half
    wait_small(i_buf, n_ce - 1, 6, small_recv)
    summed = jnp.sum(i_buf[...], axis=0)
    curvature = jnp.sum(summed[:, 2 * rows :], axis=1, keepdims=True) + ridge * dir_norm
    alpha = old_norm / curvature
    squares = jnp.zeros((1, rows), F32)
    for side in range(2):
        own_dir = a_buf[pair + 2 * side, :, 0:rows]
        image = summed[:, side * rows : (side + 1) * rows] + ridge * own_dir
        left = a_buf[pair + 2 * side, :, rows : 2 * rows] - alpha * image
        squares = squares + left * left
        left_ref[side] = left
    e_buf[mine] = squares

    @pl.loop(1, n_q)
    def _(k):
        copy_small(e_buf.at[mine], e_buf.at[mine], 7, column_peer(k)[1])

    out_ref[0:1, :] = jnp.broadcast_to(alpha, (1, rows))
    out_ref[1:2, :] = left_ref[half]
    wait_small(e_buf, n_q - 1, 7, small_recv)
    new_norm = jnp.sum(jnp.sum(e_buf[...], axis=0), axis=1, keepdims=True)
    out_ref[2:3, :] = jnp.broadcast_to(new_norm / old_norm, (1, rows))

    for slot, landing, count in (
        (0, a_buf, n_q - 1),
        (1, a_buf, 1),
        (2, a_buf, n_q - 1),
        (3, m_buf, n_ce - 1),
        (4, c_buf, n_q - 1),
        (5, g_buf, n_p - 1),
        (6, i_buf, n_ce - 1),
        (7, e_buf, n_q - 1),
    ):
        wait_small(landing, count, slot, small_send)
    sent = cen.at[pl.ds(0, n_ce - 1)]
    pltpu.make_async_copy(sent, sent, cen_send).wait()


def on_device(n_dp, n_ce, samples, centres, factor, solution, residual, direction):
    rows, depth = centres.shape
    width = samples.shape[0]
    total_samples = width * n_dp * n_ce
    scale = 1.0 / (balance * total_samples * math.sqrt(rows * n_ce))
    hbm = pl.BlockSpec(memory_space=pltpu.HBM)
    n_q = n_ce // 2
    n_p = 2 * n_dp
    out = pl.pallas_call(
        functools.partial(step_kernel, n_dp, n_ce, scale),
        out_shape=jax.ShapeDtypeStruct((8, rows), F32),
        in_specs=[hbm] * 5,
        out_specs=pl.BlockSpec(memory_space=pltpu.VMEM),
        scratch_shapes=[
            pltpu.VMEM((width, depth), BF16),
            pltpu.VMEM((n_ce, rows, depth), BF16),
            pltpu.VMEM((rows, rows * n_ce), F32),
            pltpu.VMEM((1, rows), F32),
            pltpu.VMEM((1, rows), F32),
            pltpu.VMEM((n_ce // 2, 2 * rows, width), BF16),
            pltpu.VMEM((1, width), F32),
            pltpu.VMEM((n_ce, 1, 2 * rows), F32),
            pltpu.VMEM((n_ce, 1, rows), F32),
            pltpu.VMEM((n_q, 1, 2 * rows), F32),
            pltpu.VMEM((n_q, 1, 2 * rows), F32),
            pltpu.VMEM((2, 1, rows), F32),
            pltpu.VMEM((n_p, 1, rows), F32),
            pltpu.VMEM((n_q, 1, 3 * rows), F32),
            pltpu.VMEM((n_ce, 1, 3 * rows), F32),
            pltpu.VMEM((n_q, 1, rows), F32),
            pltpu.VMEM((2, 1, rows), F32),
            pltpu.SemaphoreType.DMA((5,)),
            pltpu.SemaphoreType.DMA((n_ce + 2,)),
            pltpu.SemaphoreType.DMA,
            pltpu.SemaphoreType.DMA((8,)),
            pltpu.SemaphoreType.DMA((8,)),
            pltpu.SemaphoreType.REGULAR,
        ],
        compiler_params=pltpu.CompilerParams(
            collective_id=0, has_side_effects=True, vmem_limit_bytes=63 * 1024 * 1024
        ),
        cost_estimate=pl.CostEstimate(
            flops=2 * width * rows * n_ce * (depth + 2),
            bytes_accessed=4 * rows * rows * n_ce,
            transcendentals=width * rows * n_ce,
        ),
    )(samples, centres, factor, residual.reshape(1, rows), direction.reshape(1, rows))
    alpha, new_residual, ratio = out[0], out[1], out[2]
    return (solution + alpha * direction, new_residual, new_residual + ratio * direction)


def solution(mesh):
    return jax.shard_map(
        functools.partial(on_device, mesh.shape["dp"], mesh.shape["centre"]),
        mesh=mesh,
        in_specs=(
            P(("dp", "centre"), None),
            P("centre", None),
            P("centre", None),
            P("centre"),
            P("centre"),
            P("centre"),
        ),
        out_specs=(P("centre"), P("centre"), P("centre")),
        check_vma=False,
    )
```

```python
import functools
import math

import jax
import jax.numpy as jnp
from jax import lax
from jax.experimental import pallas as pl
from jax.experimental.pallas import tpu as pltpu
from jax.sharding import PartitionSpec as P

sharpness = 6.0
ridge = 0.3
balance = 16.0
z_low = 4
EDGES = True
MESH = pl.DeviceIdType.MESH
F32 = jnp.float32
BF16 = jnp.bfloat16


def step_kernel(
    n_dp,
    n_ce,
    scale,
    samples_hbm,
    centres_hbm,
    factor_hbm,
    res_hbm,
    dir_hbm,
    out_ref,
    smp,
    cen,
    fac,
    res_ref,
    dir_ref,
    tiles,
    row_term,
    a_buf,
    m_buf,
    c_out,
    c_buf,
    g_out,
    g_buf,
    i_out,
    i_buf,
    e_buf,
    left_ref,
    w_acc,
    load_sem,
    cen_recv,
    cen_send,
    small_recv,
    small_send,
    token,
):
    dp = lax.axis_index("dp")
    me = lax.axis_index("centre")
    rows, depth = cen.shape[1], cen.shape[2]
    width = smp.shape[0]
    n_y = n_ce // 4
    n_q = 2 * n_y
    n_x = n_dp // z_low
    n_z = 2 * z_low
    n_p = n_x * n_z
    n_tiles = n_ce // 2
    x, low_z = dp // z_low, lax.rem(dp, z_low)
    y, half, core = me // 4, lax.rem(me // 2, 2), lax.rem(me, 2)
    z = half * z_low + low_z
    mine = y * 2 + core
    place = x * n_z + z

    def column_peer(k):
        q = lax.rem(mine + k, n_q)
        return q, (dp, (q // 2) * 4 + half * 2 + lax.rem(q, 2))

    def z_peer(k):
        other = lax.rem(z + k, n_z)
        return (x * z_low + lax.rem(other, z_low), y * 4 + (other // z_low) * 2 + core)

    def plane_peer(k):
        p = lax.rem(place + k, n_p)
        other = lax.rem(p, n_z)
        there = (p // n_z) * z_low + lax.rem(other, z_low)
        return other // z_low, (there, y * 4 + (other // z_low) * 2 + core)

    def group_peer(k):
        peer = lax.rem(me + k, n_ce)
        return (peer // 4) * 2 + lax.rem(peer, 2), (dp, peer)

    up = lax.rem(me + 4, n_ce)
    down = lax.rem(me + n_ce - 4, n_ce)
    sibling = me + 1 - 2 * core
    across = me + 2 - 4 * half

    at_edge = (low_z == 0) | (low_z == z_low - 1)
    first_low = jnp.where(low_z == 0, z_low - 1, 0)
    second_low = jnp.where(low_z == 0, z_low - 2, 1)
    served = [x * z_low + first_low, x * z_low + second_low]

    loads = [
        pltpu.make_async_copy(dir_hbm, dir_ref, load_sem.at[0]),
        pltpu.make_async_copy(res_hbm, res_ref, load_sem.at[1]),
        pltpu.make_async_copy(centres_hbm, cen.at[me], load_sem.at[2]),
        pltpu.make_async_copy(samples_hbm, smp, load_sem.at[3]),
        pltpu.make_async_copy(factor_hbm, fac, load_sem.at[4]),
    ]
    for load in loads:
        load.start()

    barrier = pltpu.get_barrier_semaphore()

    @pl.loop(1, n_q)
    def _(k):
        pl.semaphore_signal(barrier, inc=1, device_id=column_peer(k)[1], device_id_type=MESH)

    @pl.loop(1, n_z)
    def _(k):
        pl.semaphore_signal(barrier, inc=1, device_id=z_peer(k), device_id_type=MESH)

    @pl.loop(1, n_x)
    def _(k):
        peer = lax.rem(x + k, n_x) * z_low + low_z
        pl.semaphore_signal(barrier, inc=1, device_id=(peer, me), device_id_type=MESH)

    def copy_small(source, target, slot, device):
        pltpu.make_async_remote_copy(
            src_ref=source,
            dst_ref=target,
            send_sem=small_send.at[slot],
            recv_sem=small_recv.at[slot],
            device_id=device,
            device_id_type=MESH,
        ).start()

    def wait_small(landing, count, slot, sems):
        part = landing.at[pl.ds(0, count)]
        pltpu.make_async_copy(part, part, sems.at[slot]).wait()

    def push_group(slot, source, landing):
        if EDGES:
            @pl.when(at_edge)
            def _():
                for there in served:

                    @pl.loop(0, n_q)
                    def _(k):
                        q = lax.rem(mine + k + n_q // 2, n_q)
                        peer = (q // 2) * 4 + (1 - half) * 2 + lax.rem(q, 2)
                        copy_small(source(q), landing.at[me], slot, (there, peer))

            @pl.loop(1, n_q)
            def _(k):
                q, device = column_peer(k)
                copy_small(source(q), landing.at[me], slot, device)
        else:

            @pl.loop(1, n_ce)
            def _(k):
                q, device = group_peer(k)
                copy_small(source(q), landing.at[me], slot, device)

    def send_cen(slot, peer, part=slice(None), sem=None, there=dp, sent_sem=0):
        pltpu.make_async_remote_copy(
            src_ref=centres_hbm if slot is me else cen.at[slot, part],
            dst_ref=cen.at[slot, part],
            send_sem=cen_send.at[sent_sem],
            recv_sem=cen_recv.at[slot if sem is None else sem],
            device_id=(there, peer),
            device_id_type=MESH,
        ).start()

    def wait_cen(slot, part=slice(None), sem=None):
        landed = cen.at[slot, part]
        pltpu.make_async_copy(
            landed, landed, cen_recv.at[slot if sem is None else sem]
        ).wait()

    loads[0].wait()
    loads[1].wait()
    a_buf[me, :, 0:rows] = dir_ref[...]
    a_buf[me, :, rows : 2 * rows] = res_ref[...]
    pl.semaphore_wait(barrier, n_q + n_z + n_x - 3)

    @pl.when(at_edge)
    def _():
        for there in served:
            copy_small(a_buf.at[me], a_buf.at[me], 1, (there, across))

    @pl.loop(1, n_q)
    def _(k):
        copy_small(a_buf.at[me], a_buf.at[me], 0, column_peer(k)[1])

    @pl.when(at_edge)
    def _():
        for there in served:
            send_cen(me, across, there=there, sent_sem=1)

    send_cen(me, up)
    send_cen(me, down)
    send_cen(me, sibling)

    @pl.loop(1, n_z)
    def _(k):
        pl.semaphore_signal(token, inc=1, device_id=z_peer(k), device_id_type=MESH)

    log2e = math.log2(math.e)
    unit = sharpness / depth * log2e
    loads[3].wait()
    for part in range(width // rows):
        block = smp[part * rows : (part + 1) * rows, :].astype(F32)
        square = block * block
        folded = square[:, 0:rows]
        for other in range(1, depth // rows):
            folded = folded + square[:, other * rows : (other + 1) * rows]
        norms = jnp.sum(folded.T, axis=0, keepdims=True)
        row_term[:, part * rows : (part + 1) * rows] = (2.0 * sharpness * log2e) - unit * norms
    loads[2].wait()

    def make_tile(slot):
        tile = slot // 2
        block = cen[pl.ds(2 * tile, 2)].reshape(2 * rows, depth)
        wide = block.astype(F32)
        norms = jnp.sum(wide * wide, axis=1, keepdims=True) * unit
        cross = lax.dot_general(
            block, smp[...], (((1,), (1,)), ((), ())), preferred_element_type=F32
        )
        power = cross * (2.0 * unit) + (row_term[...] - norms)
        tiles[tile] = jnp.exp2(power).astype(BF16)

    def twin(slot):
        return slot + 1 - 2 * core

    top, bottom = slice(0, rows // 2), slice(rows // 2, rows)
    up_two = lax.rem(me + 8, n_ce)
    down_two = lax.rem(me + n_ce - 8, n_ce)

    def ends(first, s):
        return lax.rem(first + n_ce - 4 * s, n_ce), lax.rem(first + 4 * s, n_ce)

    def pull_own(s):
        low, high = ends(me, s)
        wait_cen(low)
        if s < n_y // 2 - 1:
            send_cen(low, up)
        else:
            send_cen(low, up, top)
        send_cen(low, sibling)
        wait_cen(high)
        if s < n_y // 2 - 1:
            send_cen(high, down)
        else:
            send_cen(high, down, bottom, n_ce)
        send_cen(high, sibling)
        return [low, high]

    def pull_across(s):
        low, high = ends(across, s)
        wait_cen(low)
        if s == 2:
            send_cen(low, up_two, top)
            send_cen(low, up)
        send_cen(low, sibling)
        wait_cen(high)
        if s == 2:
            send_cen(high, down_two, bottom, n_ce + 1)
            send_cen(high, down)
        send_cen(high, sibling)
        return [low, high]

    def pull_far(first, sem):
        far = lax.rem(first + n_ce // 2, n_ce)
        wait_cen(far, top)
        wait_cen(far, bottom, sem)
        send_cen(far, sibling)
        return [far]

    def work(slots):
        for slot in slots:
            wait_cen(twin(slot))
            make_tile(slot)

    work([me])
    wait_small(a_buf, 1, 1, small_recv)

    @pl.loop(1, n_q)
    def _(k):
        copy_small(a_buf.at[across], a_buf.at[across], 2, column_peer(k)[1])

    wait_cen(across)
    send_cen(across, up_two)
    send_cen(across, down_two)
    send_cen(across, up)
    send_cen(across, down)
    send_cen(across, sibling)
    near = pull_own(1)
    work([across])
    next_own = pull_own(2)
    work(near)

    wait_small(a_buf, n_q - 1, 0, small_recv)
    wait_small(a_buf, n_q - 1, 2, small_recv)
    loads[4].wait()
    acc = fac[:, 0:rows] * a_buf[0, :, 0:rows]
    for b in range(1, n_ce):
        acc = acc + fac[:, b * rows : (b + 1) * rows] * a_buf[b, :, 0:rows]
    m_buf[me] = jnp.sum(acc.T, axis=0, keepdims=True)
    push_group(3, lambda q: m_buf.at[me], m_buf)

    next_far = pull_across(2)
    work(next_own)
    last_far = pull_across(1)
    work(next_far)
    farther = pull_own(3)
    work(last_far)

    wait_small(m_buf, n_ce - 1, 3, small_recv)
    w_acc[...] = jnp.zeros_like(w_acc)

    def weigh(slots):
        total = w_acc[...]
        for slot in slots:
            tile = slot // 2
            coeffs = jnp.concatenate([m_buf[2 * tile], m_buf[2 * tile + 1]], axis=1)
            coeffs = jnp.broadcast_to(coeffs, (16, 2 * rows)).astype(BF16)
            total = total + jnp.dot(coeffs, tiles[tile], preferred_element_type=F32)
        w_acc[...] = total

    weigh([me, across] + near)
    last_own = pull_across(3)
    work(farther)
    weigh(next_own + next_far)
    far_across = pull_far(across, n_ce + 1)
    work(last_own)
    weigh(last_far + farther)
    far_own = pull_far(me, n_ce)
    work(far_across)
    weigh(last_own + far_across)
    work(far_own)
    weigh(far_own)

    weights = w_acc[...]
    upright = jnp.broadcast_to(weights[0:1], (rows, width)).T.astype(BF16)
    diagonal = lax.broadcasted_iota(jnp.int32, (rows, rows), 0) == lax.broadcasted_iota(
        jnp.int32, (rows, rows), 1
    )

    across_row = weights[0:1].astype(BF16).astype(F32)

    @pl.loop(0, n_y)
    def _(row):
        part = jnp.dot(tiles[2 * row], upright, preferred_element_type=F32)
        for c in range(2):
            picked = jnp.where(diagonal, part[c * rows : (c + 1) * rows], 0.0)
            c_out[2 * row + c, :, 0:rows] = jnp.sum(picked, axis=0, keepdims=True)
            block = tiles[2 * row + 1, c * rows : (c + 1) * rows, :]
            acc = block[:, 0:rows].astype(F32) * across_row[:, 0:rows]
            for p in range(1, width // rows):
                cut = slice(p * rows, (p + 1) * rows)
                acc = acc + block[:, cut].astype(F32) * across_row[:, cut]
            c_out[2 * row + c, :, rows : 2 * rows] = jnp.sum(acc.T, axis=0, keepdims=True)

    c_buf[mine] = c_out[mine]

    @pl.loop(1, n_q)
    def _(k):
        q, device = column_peer(k)
        copy_small(c_out.at[q], c_buf.at[mine], 4, device)

    wait_small(c_buf, n_q - 1, 4, small_recv)
    both = jnp.sum(c_buf[...], axis=0)
    g_out[0] = both[:, 0:rows]
    g_out[1] = both[:, rows : 2 * rows]
    pl.semaphore_wait(token, n_z - 1)

    @pl.loop(1, n_p)
    def _(k):
        side, device = plane_peer(k)
        copy_small(g_out.at[side], g_buf.at[place], 5, device)

    g_buf[place] = g_out[half]
    wait_small(g_buf, n_p - 1, 5, small_recv)
    columns = jnp.sum(g_buf[...], axis=0) * scale

    spread = jnp.broadcast_to(columns, (rows, rows)).T
    bend = m_buf[me] * columns
    for b in range(n_ce):
        i_out[b // 4, :, (b % 4) * rows : (b % 4 + 1) * rows] = jnp.sum(
            fac[:, b * rows : (b + 1) * rows] * spread, axis=0, keepdims=True
        )
    for b in range(n_y):
        i_out[b, :, 4 * rows : 5 * rows] = bend

    push_group(6, lambda q: i_out.at[q // 2], i_buf)

    i_buf[me] = i_out[y]
    whole_dir = a_buf[:, :, 0:rows]
    whole_res = a_buf[:, :, rows : 2 * rows]
    dir_norm = jnp.sum(jnp.sum(whole_dir * whole_dir, axis=0), axis=1, keepdims=True)
    old_norm = jnp.sum(jnp.sum(whole_res * whole_res, axis=0), axis=1, keepdims=True)
    wait_small(i_buf, n_ce - 1, 6, small_recv)
    summed = jnp.sum(i_buf[...], axis=0)
    curvature = jnp.sum(summed[:, 4 * rows :], axis=1, keepdims=True) + ridge * dir_norm
    alpha = old_norm / curvature
    squares = jnp.zeros((1, rows), F32)
    for b in range(4):
        own_dir = a_buf[4 * y + b, :, 0:rows]
        image = summed[:, b * rows : (b + 1) * rows] + ridge * own_dir
        left = a_buf[4 * y + b, :, rows : 2 * rows] - alpha * image
        squares = squares + left * left
        left_ref[b] = left
    e_buf[y] = squares

    @pl.loop(1, n_y)
    def _(k):
        peer = lax.rem(me + 4 * k, n_ce)
        copy_small(e_buf.at[y], e_buf.at[y], 7, (dp, peer))

    out_ref[0:1, :] = jnp.broadcast_to(alpha, (1, rows))
    out_ref[1:2, :] = left_ref[me - 4 * y]
    wait_small(e_buf, n_y - 1, 7, small_recv)
    new_norm = jnp.sum(jnp.sum(e_buf[...], axis=0), axis=1, keepdims=True)
    out_ref[2:3, :] = jnp.broadcast_to(new_norm / old_norm, (1, rows))

    for slot, landing, count in (
        (0, a_buf, n_q - 1),
        (2, a_buf, n_q - 1),
        (3, m_buf, n_q - 1 if EDGES else n_ce - 1),
        (4, c_buf, n_q - 1),
        (5, g_buf, n_p - 1),
        (6, i_buf, n_q - 1 if EDGES else n_ce - 1),
        (7, e_buf, n_y - 1),
    ):
        wait_small(landing, count, slot, small_send)

    @pl.when(at_edge)
    def _():
        wait_small(a_buf, 2, 1, small_send)
        if EDGES:
            wait_small(m_buf, n_ce, 3, small_send)
            wait_small(i_buf, n_ce, 6, small_send)
        crossed = cen.at[pl.ds(0, 2)]
        pltpu.make_async_copy(crossed, crossed, cen_send.at[1]).wait()

    sent = cen.at[pl.ds(0, n_ce - 2)]
    pltpu.make_async_copy(sent, sent, cen_send.at[0]).wait()


def on_device(n_dp, n_ce, samples, centres, factor, solution, residual, direction):
    rows, depth = centres.shape
    width = samples.shape[0]
    total_samples = width * n_dp * n_ce
    scale = 1.0 / (balance * total_samples * math.sqrt(rows * n_ce))
    hbm = pl.BlockSpec(memory_space=pltpu.HBM)
    n_q = n_ce // 2
    n_p = 2 * n_dp
    out = pl.pallas_call(
        functools.partial(step_kernel, n_dp, n_ce, scale),
        out_shape=jax.ShapeDtypeStruct((8, rows), F32),
        in_specs=[hbm] * 5,
        out_specs=pl.BlockSpec(memory_space=pltpu.VMEM),
        scratch_shapes=[
            pltpu.VMEM((width, depth), BF16),
            pltpu.VMEM((n_ce, rows, depth), BF16),
            pltpu.VMEM((rows, rows * n_ce), F32),
            pltpu.VMEM((1, rows), F32),
            pltpu.VMEM((1, rows), F32),
            pltpu.VMEM((n_ce // 2, 2 * rows, width), BF16),
            pltpu.VMEM((1, width), F32),
            pltpu.VMEM((n_ce, 1, 2 * rows), F32),
            pltpu.VMEM((n_ce, 1, rows), F32),
            pltpu.VMEM((n_q, 1, 2 * rows), F32),
            pltpu.VMEM((n_q, 1, 2 * rows), F32),
            pltpu.VMEM((2, 1, rows), F32),
            pltpu.VMEM((n_p, 1, rows), F32),
            pltpu.VMEM((n_ce // 4, 1, 5 * rows), F32),
            pltpu.VMEM((n_ce, 1, 5 * rows), F32),
            pltpu.VMEM((n_ce // 4, 1, rows), F32),
            pltpu.VMEM((4, 1, rows), F32),
            pltpu.VMEM((16, width), F32),
            pltpu.SemaphoreType.DMA((5,)),
            pltpu.SemaphoreType.DMA((n_ce + 2,)),
            pltpu.SemaphoreType.DMA((2,)),
            pltpu.SemaphoreType.DMA((8,)),
            pltpu.SemaphoreType.DMA((8,)),
            pltpu.SemaphoreType.REGULAR,
        ],
        compiler_params=pltpu.CompilerParams(
            collective_id=0, has_side_effects=True, vmem_limit_bytes=63 * 1024 * 1024
        ),
        cost_estimate=pl.CostEstimate(
            flops=2 * width * rows * n_ce * (depth + 2),
            bytes_accessed=4 * rows * rows * n_ce,
            transcendentals=width * rows * n_ce,
        ),
    )(samples, centres, factor, residual.reshape(1, rows), direction.reshape(1, rows))
    alpha, new_residual, ratio = out[0], out[1], out[2]
    return (solution + alpha * direction, new_residual, new_residual + ratio * direction)


def solution(mesh):
    return jax.shard_map(
        functools.partial(on_device, mesh.shape["dp"], mesh.shape["centre"]),
        mesh=mesh,
        in_specs=(
            P(("dp", "centre"), None),
            P("centre", None),
            P("centre", None),
            P("centre"),
            P("centre"),
            P("centre"),
        ),
        out_specs=(P("centre"), P("centre"), P("centre")),
        check_vma=False,
    )
```

```python
import functools
import math

import jax
import jax.numpy as jnp
from jax import lax
from jax.experimental import pallas as pl
from jax.experimental.pallas import tpu as pltpu
from jax.sharding import PartitionSpec as P

sharpness = 6.0
ridge = 0.3
balance = 16.0
z_low = 4
MESH = pl.DeviceIdType.MESH
F32 = jnp.float32
BF16 = jnp.bfloat16


def step_kernel(
    n_dp,
    n_ce,
    scale,
    samples_hbm,
    centres_hbm,
    factor_hbm,
    res_hbm,
    dir_hbm,
    out_ref,
    smp,
    cen,
    fac,
    res_ref,
    dir_ref,
    tiles,
    row_term,
    a_buf,
    m_buf,
    c_out,
    c_buf,
    g_out,
    g_buf,
    i_out,
    i_buf,
    e_buf,
    left_ref,
    w_acc,
    load_sem,
    cen_recv,
    cen_send,
    small_recv,
    small_send,
    token,
):
    dp = lax.axis_index("dp")
    me = lax.axis_index("centre")
    rows, depth = cen.shape[1], cen.shape[2]
    width = smp.shape[0]
    n_y = n_ce // 4
    n_q = 2 * n_y
    n_x = n_dp // z_low
    n_z = 2 * z_low
    n_p = n_x * n_z
    n_tiles = n_ce // 2
    x, low_z = dp // z_low, lax.rem(dp, z_low)
    y, half, core = me // 4, lax.rem(me // 2, 2), lax.rem(me, 2)
    z = half * z_low + low_z
    mine = y * 2 + core
    place = x * n_z + z

    def column_peer(k):
        q = lax.rem(mine + k, n_q)
        return q, (dp, (q // 2) * 4 + half * 2 + lax.rem(q, 2))

    def y_peer(k):
        return (dp, lax.rem(me + 4 * k, n_ce))

    def z_peer(k):
        other = lax.rem(z + k, n_z)
        return (x * z_low + lax.rem(other, z_low), y * 4 + (other // z_low) * 2 + core)

    def plane_peer(k):
        p = lax.rem(place + k, n_p)
        other = lax.rem(p, n_z)
        there = (p // n_z) * z_low + lax.rem(other, z_low)
        return other // z_low, (there, y * 4 + (other // z_low) * 2 + core)

    up = lax.rem(me + 4, n_ce)
    down = lax.rem(me + n_ce - 4, n_ce)
    sibling = me + 1 - 2 * core
    across = me + 2 - 4 * half

    at_edge = (low_z == 0) | (low_z == z_low - 1)
    first_low = jnp.where(low_z == 0, z_low - 1, 0)
    second_low = jnp.where(low_z == 0, z_low - 2, 1)
    served = [x * z_low + first_low, x * z_low + second_low]

    loads = [
        pltpu.make_async_copy(dir_hbm, dir_ref, load_sem.at[0]),
        pltpu.make_async_copy(res_hbm, res_ref, load_sem.at[1]),
        pltpu.make_async_copy(centres_hbm, cen.at[me], load_sem.at[2]),
        pltpu.make_async_copy(samples_hbm, smp, load_sem.at[3]),
        pltpu.make_async_copy(factor_hbm, fac, load_sem.at[4]),
    ]
    for load in loads:
        load.start()

    barrier = pltpu.get_barrier_semaphore()
    pl.semaphore_signal(barrier, inc=1, device_id=(dp, sibling), device_id_type=MESH)

    @pl.loop(1, n_y)
    def _(k):
        pl.semaphore_signal(barrier, inc=1, device_id=y_peer(k), device_id_type=MESH)

    @pl.loop(1, n_z)
    def _(k):
        pl.semaphore_signal(barrier, inc=1, device_id=z_peer(k), device_id_type=MESH)

    @pl.loop(1, n_x)
    def _(k):
        peer = lax.rem(x + k, n_x) * z_low + low_z
        pl.semaphore_signal(barrier, inc=1, device_id=(peer, me), device_id_type=MESH)

    def copy_small(source, target, slot, device):
        pltpu.make_async_remote_copy(
            src_ref=source,
            dst_ref=target,
            send_sem=small_send.at[slot],
            recv_sem=small_recv.at[slot],
            device_id=device,
            device_id_type=MESH,
        ).start()

    def wait_small(landing, count, slot, sems):
        part = landing.at[pl.ds(0, count)]
        pltpu.make_async_copy(part, part, sems.at[slot]).wait()

    def push_group(slot, source, landing):
        @pl.when(at_edge)
        def _():
            for there in served:

                @pl.loop(0, n_q)
                def _(k):
                    q = lax.rem(mine + k + n_q // 2, n_q)
                    peer = (q // 2) * 4 + (1 - half) * 2 + lax.rem(q, 2)
                    copy_small(source(q), landing.at[me], slot, (there, peer))

        @pl.loop(1, n_q)
        def _(k):
            q, device = column_peer(k)
            copy_small(source(q), landing.at[me], slot, device)

    def send_cen(slot, peer, part=slice(None), sem=None, there=dp, sent_sem=0):
        pltpu.make_async_remote_copy(
            src_ref=centres_hbm if slot is me else cen.at[slot, part],
            dst_ref=cen.at[slot, part],
            send_sem=cen_send.at[sent_sem],
            recv_sem=cen_recv.at[slot if sem is None else sem],
            device_id=(there, peer),
            device_id_type=MESH,
        ).start()

    def wait_cen(slot, part=slice(None), sem=None):
        landed = cen.at[slot, part]
        pltpu.make_async_copy(
            landed, landed, cen_recv.at[slot if sem is None else sem]
        ).wait()

    loads[0].wait()
    loads[1].wait()
    a_buf[me, :, 0:rows] = dir_ref[...]
    a_buf[me, :, rows : 2 * rows] = res_ref[...]
    pl.semaphore_wait(barrier, n_y + n_z + n_x - 2)

    @pl.when(at_edge)
    def _():
        for there in served:
            copy_small(a_buf.at[me], a_buf.at[me], 1, (there, across))

    @pl.loop(1, n_y)
    def _(k):
        copy_small(a_buf.at[me], a_buf.at[me], 0, y_peer(k))

    @pl.when(at_edge)
    def _():
        for there in served:
            send_cen(me, across, there=there, sent_sem=1)

    send_cen(me, up)
    send_cen(me, down)
    send_cen(me, sibling)

    @pl.loop(1, n_z)
    def _(k):
        pl.semaphore_signal(token, inc=1, device_id=z_peer(k), device_id_type=MESH)

    log2e = math.log2(math.e)
    unit = sharpness / depth * log2e
    loads[3].wait()
    for part in range(width // rows):
        block = smp[part * rows : (part + 1) * rows, :].astype(F32)
        square = block * block
        folded = square[:, 0:rows]
        for other in range(1, depth // rows):
            folded = folded + square[:, other * rows : (other + 1) * rows]
        norms = jnp.sum(folded.T, axis=0, keepdims=True)
        row_term[:, part * rows : (part + 1) * rows] = (2.0 * sharpness * log2e) - unit * norms
    loads[2].wait()

    def make_tile(slot):
        tile = slot // 2
        block = cen[pl.ds(2 * tile, 2)].reshape(2 * rows, depth)
        wide = block.astype(F32)
        norms = jnp.sum(wide * wide, axis=1, keepdims=True) * unit
        cross = lax.dot_general(
            block, smp[...], (((1,), (1,)), ((), ())), preferred_element_type=F32
        )
        power = cross * (2.0 * unit) + (row_term[...] - norms)
        tiles[tile] = jnp.exp2(power).astype(BF16)

    def twin(slot):
        return slot + 1 - 2 * core

    top, bottom = slice(0, rows // 2), slice(rows // 2, rows)
    up_two = lax.rem(me + 8, n_ce)
    down_two = lax.rem(me + n_ce - 8, n_ce)

    def ends(first, s):
        return lax.rem(first + n_ce - 4 * s, n_ce), lax.rem(first + 4 * s, n_ce)

    def pull_own(s):
        low, high = ends(me, s)
        wait_cen(low)
        if s < n_y // 2 - 1:
            send_cen(low, up)
        else:
            send_cen(low, up, top)
        send_cen(low, sibling)
        wait_cen(high)
        if s < n_y // 2 - 1:
            send_cen(high, down)
        else:
            send_cen(high, down, bottom, n_ce)
        send_cen(high, sibling)
        return [low, high]

    def pull_across(s):
        low, high = ends(across, s)
        wait_cen(low)
        if s == 2:
            send_cen(low, up_two, top)
            send_cen(low, up)
        send_cen(low, sibling)
        wait_cen(high)
        if s == 2:
            send_cen(high, down_two, bottom, n_ce + 1)
            send_cen(high, down)
        send_cen(high, sibling)
        return [low, high]

    def pull_far(first, sem):
        far = lax.rem(first + n_ce // 2, n_ce)
        wait_cen(far, top)
        wait_cen(far, bottom, sem)
        send_cen(far, sibling)
        return [far]

    def work(slots):
        for slot in slots:
            wait_cen(twin(slot))
            make_tile(slot)

    work([me])
    wait_small(a_buf, 1, 1, small_recv)

    @pl.loop(1, n_y)
    def _(k):
        copy_small(a_buf.at[across], a_buf.at[across], 2, y_peer(k))

    wait_cen(across)
    send_cen(across, up_two)
    send_cen(across, down_two)
    send_cen(across, up)
    send_cen(across, down)
    send_cen(across, sibling)
    near = pull_own(1)
    work([across] + near)
    wait_small(a_buf, n_y - 1, 0, small_recv)
    wait_small(a_buf, n_y - 1, 2, small_recv)

    @pl.loop(0, n_q)
    def _(k):
        copy_small(a_buf.at[2 * k + core], a_buf.at[2 * k + core], 8, (dp, sibling))

    next_own = pull_own(2)
    next_far = pull_across(2)

    wait_small(a_buf, n_q, 8, small_recv)
    loads[4].wait()
    acc = fac[:, 0:rows] * a_buf[0, :, 0:rows]
    for b in range(1, n_ce):
        acc = acc + fac[:, b * rows : (b + 1) * rows] * a_buf[b, :, 0:rows]
    m_buf[me] = jnp.sum(acc.T, axis=0, keepdims=True)
    push_group(3, lambda q: m_buf.at[me], m_buf)

    last_far = pull_across(1)
    work(next_own)
    farther = pull_own(3)
    work(next_far + last_far)
    last_own = pull_across(3)
    work(farther)
    far_across = pull_far(across, n_ce + 1)
    work(last_own)

    wait_small(m_buf, n_ce - 1, 3, small_recv)

    def weigh(slots, start=False):
        total = jnp.zeros_like(w_acc) if start else w_acc[...]
        for slot in slots:
            tile = slot // 2
            coeffs = jnp.concatenate([m_buf[2 * tile], m_buf[2 * tile + 1]], axis=1)
            coeffs = jnp.broadcast_to(coeffs, (16, 2 * rows)).astype(BF16)
            total = total + jnp.dot(coeffs, tiles[tile], preferred_element_type=F32)
        w_acc[...] = total

    weigh([me, across] + near + next_own + next_far, True)
    far_own = pull_far(me, n_ce)
    work(far_across)
    weigh(last_far + farther + last_own)
    work(far_own)
    weigh(far_across + far_own)
    weights = w_acc[...]
    upright = jnp.broadcast_to(weights[0:1], (rows, width)).T.astype(BF16)
    diagonal = lax.broadcasted_iota(jnp.int32, (rows, rows), 0) == lax.broadcasted_iota(
        jnp.int32, (rows, rows), 1
    )

    across_row = weights[0:1].astype(BF16).astype(F32)

    def far_first(k):
        return lax.rem(y + n_y // 2 + (k + 1) // 2 * (1 - 2 * lax.rem(k, 2)), n_y)

    @pl.loop(0, n_y)
    def _(k):
        row = far_first(k)
        part = jnp.dot(tiles[2 * row], upright, preferred_element_type=F32)
        for c in range(2):
            picked = jnp.where(diagonal, part[c * rows : (c + 1) * rows], 0.0)
            c_out[2 * row + c, :, 0:rows] = jnp.sum(picked, axis=0, keepdims=True)
            block = tiles[2 * row + 1, c * rows : (c + 1) * rows, :]
            acc = block[:, 0:rows].astype(F32) * across_row[:, 0:rows]
            for p in range(1, width // rows):
                cut = slice(p * rows, (p + 1) * rows)
                acc = acc + block[:, cut].astype(F32) * across_row[:, cut]
            c_out[2 * row + c, :, rows : 2 * rows] = jnp.sum(acc.T, axis=0, keepdims=True)
        there = row * 4 + half * 2
        copy_small(c_out.at[2 * row + 1 - core], c_buf.at[mine], 4, (dp, there + 1 - core))

        @pl.when(row != y)
        def _():
            copy_small(c_out.at[2 * row + core], c_buf.at[mine], 4, (dp, there + core))

    c_buf[mine] = c_out[mine]
    wait_small(c_buf, n_q - 1, 4, small_recv)
    both = jnp.sum(c_buf[...], axis=0)
    g_out[0] = both[:, 0:rows]
    g_out[1] = both[:, rows : 2 * rows]
    pl.semaphore_wait(token, n_z - 1)

    @pl.loop(1, n_p)
    def _(k):
        side, device = plane_peer(k)
        copy_small(g_out.at[side], g_buf.at[place], 5, device)

    g_buf[place] = g_out[half]
    wait_small(g_buf, n_p - 1, 5, small_recv)
    columns = jnp.sum(g_buf[...], axis=0) * scale

    spread = jnp.broadcast_to(columns, (rows, rows)).T
    bend = m_buf[me] * columns
    @pl.loop(0, n_y)
    def _(k):
        row = far_first(k)
        for b in range(4):
            start = pl.multiple_of((4 * row + b) * rows, rows)
            i_out[row, :, b * rows : (b + 1) * rows] = jnp.sum(
                fac[:, pl.ds(start, rows)] * spread, axis=0, keepdims=True
            )
        i_out[row, :, 4 * rows : 5 * rows] = bend

        @pl.when(at_edge)
        def _():
            for there in served:
                for c in range(2):
                    peer = row * 4 + (1 - half) * 2 + c
                    copy_small(i_out.at[row], i_buf.at[me], 6, (there, peer))

        near_by = row * 4 + half * 2
        copy_small(i_out.at[row], i_buf.at[me], 6, (dp, near_by + 1 - core))

        @pl.when(row != y)
        def _():
            copy_small(i_out.at[row], i_buf.at[me], 6, (dp, near_by + core))

    i_buf[me] = i_out[y]
    whole_dir = a_buf[:, :, 0:rows]
    whole_res = a_buf[:, :, rows : 2 * rows]
    dir_norm = jnp.sum(jnp.sum(whole_dir * whole_dir, axis=0), axis=1, keepdims=True)
    old_norm = jnp.sum(jnp.sum(whole_res * whole_res, axis=0), axis=1, keepdims=True)
    wait_small(i_buf, n_ce - 1, 6, small_recv)
    summed = jnp.sum(i_buf[...], axis=0)
    curvature = jnp.sum(summed[:, 4 * rows :], axis=1, keepdims=True) + ridge * dir_norm
    alpha = old_norm / curvature
    squares = jnp.zeros((1, rows), F32)
    for b in range(4):
        own_dir = a_buf[4 * y + b, :, 0:rows]
        image = summed[:, b * rows : (b + 1) * rows] + ridge * own_dir
        left = a_buf[4 * y + b, :, rows : 2 * rows] - alpha * image
        squares = squares + left * left
        left_ref[b] = left
    e_buf[y] = squares

    @pl.loop(1, n_y)
    def _(k):
        peer = lax.rem(me + 4 * k, n_ce)
        copy_small(e_buf.at[y], e_buf.at[y], 7, (dp, peer))

    out_ref[0:1, :] = jnp.broadcast_to(alpha, (1, rows))
    out_ref[1:2, :] = left_ref[me - 4 * y]
    wait_small(e_buf, n_y - 1, 7, small_recv)
    new_norm = jnp.sum(jnp.sum(e_buf[...], axis=0), axis=1, keepdims=True)
    out_ref[2:3, :] = jnp.broadcast_to(new_norm / old_norm, (1, rows))

    for slot, landing, count in (
        (0, a_buf, n_y - 1),
        (2, a_buf, n_y - 1),
        (8, a_buf, n_q),
        (3, m_buf, n_q - 1),
        (4, c_buf, n_q - 1),
        (5, g_buf, n_p - 1),
        (6, i_buf, n_q - 1),
        (7, e_buf, n_y - 1),
    ):
        wait_small(landing, count, slot, small_send)

    @pl.when(at_edge)
    def _():
        wait_small(a_buf, 2, 1, small_send)
        wait_small(m_buf, n_ce, 3, small_send)
        wait_small(i_buf, n_ce, 6, small_send)
        crossed = cen.at[pl.ds(0, 2)]
        pltpu.make_async_copy(crossed, crossed, cen_send.at[1]).wait()

    sent = cen.at[pl.ds(0, n_ce - 2)]
    pltpu.make_async_copy(sent, sent, cen_send.at[0]).wait()


def on_device(n_dp, n_ce, samples, centres, factor, solution, residual, direction):
    rows, depth = centres.shape
    width = samples.shape[0]
    total_samples = width * n_dp * n_ce
    scale = 1.0 / (balance * total_samples * math.sqrt(rows * n_ce))
    hbm = pl.BlockSpec(memory_space=pltpu.HBM)
    n_q = n_ce // 2
    n_p = 2 * n_dp
    out = pl.pallas_call(
        functools.partial(step_kernel, n_dp, n_ce, scale),
        out_shape=jax.ShapeDtypeStruct((8, rows), F32),
        in_specs=[hbm] * 5,
        out_specs=pl.BlockSpec(memory_space=pltpu.VMEM),
        scratch_shapes=[
            pltpu.VMEM((width, depth), BF16),
            pltpu.VMEM((n_ce, rows, depth), BF16),
            pltpu.VMEM((rows, rows * n_ce), F32),
            pltpu.VMEM((1, rows), F32),
            pltpu.VMEM((1, rows), F32),
            pltpu.VMEM((n_ce // 2, 2 * rows, width), BF16),
            pltpu.VMEM((1, width), F32),
            pltpu.VMEM((n_ce, 1, 2 * rows), F32),
            pltpu.VMEM((n_ce, 1, rows), F32),
            pltpu.VMEM((n_q, 1, 2 * rows), F32),
            pltpu.VMEM((n_q, 1, 2 * rows), F32),
            pltpu.VMEM((2, 1, rows), F32),
            pltpu.VMEM((n_p, 1, rows), F32),
            pltpu.VMEM((n_ce // 4, 1, 5 * rows), F32),
            pltpu.VMEM((n_ce, 1, 5 * rows), F32),
            pltpu.VMEM((n_ce // 4, 1, rows), F32),
            pltpu.VMEM((4, 1, rows), F32),
            pltpu.VMEM((16, width), F32),
            pltpu.SemaphoreType.DMA((5,)),
            pltpu.SemaphoreType.DMA((n_ce + 2,)),
            pltpu.SemaphoreType.DMA((2,)),
            pltpu.SemaphoreType.DMA((9,)),
            pltpu.SemaphoreType.DMA((9,)),
            pltpu.SemaphoreType.REGULAR,
        ],
        compiler_params=pltpu.CompilerParams(
            collective_id=0, has_side_effects=True, vmem_limit_bytes=63 * 1024 * 1024
        ),
        cost_estimate=pl.CostEstimate(
            flops=2 * width * rows * n_ce * (depth + 2),
            bytes_accessed=4 * rows * rows * n_ce,
            transcendentals=width * rows * n_ce,
        ),
    )(samples, centres, factor, residual.reshape(1, rows), direction.reshape(1, rows))
    alpha, new_residual, ratio = out[0], out[1], out[2]
    return (solution + alpha * direction, new_residual, new_residual + ratio * direction)


def solution(mesh):
    return jax.shard_map(
        functools.partial(on_device, mesh.shape["dp"], mesh.shape["centre"]),
        mesh=mesh,
        in_specs=(
            P(("dp", "centre"), None),
            P("centre", None),
            P("centre", None),
            P("centre"),
            P("centre"),
            P("centre"),
        ),
        out_specs=(P("centre"), P("centre"), P("centre")),
        check_vma=False,
    )
```

```python
import functools
import math

import jax
import jax.numpy as jnp
from jax import lax
from jax.experimental import pallas as pl
from jax.experimental.pallas import tpu as pltpu
from jax.sharding import PartitionSpec as P

sharpness = 6.0
ridge = 0.3
balance = 16.0
z_low = 4
MESH = pl.DeviceIdType.MESH
F32 = jnp.float32
BF16 = jnp.bfloat16


def step_kernel(
    n_dp,
    n_ce,
    scale,
    samples_hbm,
    centres_hbm,
    factor_hbm,
    res_hbm,
    dir_hbm,
    out_ref,
    smp,
    cen,
    fac,
    res_ref,
    dir_ref,
    tiles,
    row_term,
    a_buf,
    m_buf,
    c_out,
    c_buf,
    g_out,
    g_buf,
    i_out,
    i_buf,
    e_buf,
    left_ref,
    w_acc,
    load_sem,
    cen_recv,
    cen_send,
    small_recv,
    small_send,
    token,
):
    dp = lax.axis_index("dp")
    me = lax.axis_index("centre")
    rows, depth = cen.shape[1], cen.shape[2]
    width = smp.shape[0]
    n_y = n_ce // 4
    n_q = 2 * n_y
    n_x = n_dp // z_low
    n_z = 2 * z_low
    n_p = n_x * n_z
    n_tiles = n_ce // 2
    x, low_z = dp // z_low, lax.rem(dp, z_low)
    y, half, core = me // 4, lax.rem(me // 2, 2), lax.rem(me, 2)
    z = half * z_low + low_z
    mine = y * 2 + core
    place = x * n_z + z

    def column_peer(k):
        q = lax.rem(mine + k, n_q)
        return q, (dp, (q // 2) * 4 + half * 2 + lax.rem(q, 2))

    def y_peer(k):
        return (dp, lax.rem(me + 4 * k, n_ce))

    def z_peer(k):
        other = lax.rem(z + k, n_z)
        return (x * z_low + lax.rem(other, z_low), y * 4 + (other // z_low) * 2 + core)

    def plane_peer(k):
        step = k // n_x
        move = n_z // 2 + (step + 1) // 2 * (1 - 2 * lax.rem(step, 2))
        other = lax.rem(z + move, n_z)
        other_x = lax.rem(x + lax.rem(k, n_x) + 1, n_x)
        there = other_x * z_low + lax.rem(other, z_low)
        return other // z_low, (there, y * 4 + (other // z_low) * 2 + core)

    up = lax.rem(me + 4, n_ce)
    down = lax.rem(me + n_ce - 4, n_ce)
    sibling = me + 1 - 2 * core
    across = me + 2 - 4 * half

    at_edge = (low_z == 0) | (low_z == z_low - 1)
    first_low = jnp.where(low_z == 0, z_low - 1, 0)
    second_low = jnp.where(low_z == 0, z_low - 2, 1)
    served = [x * z_low + first_low, x * z_low + second_low]

    loads = [
        pltpu.make_async_copy(dir_hbm, dir_ref, load_sem.at[0]),
        pltpu.make_async_copy(res_hbm, res_ref, load_sem.at[1]),
        pltpu.make_async_copy(centres_hbm, cen.at[me], load_sem.at[2]),
        pltpu.make_async_copy(samples_hbm, smp, load_sem.at[3]),
        pltpu.make_async_copy(factor_hbm, fac, load_sem.at[4]),
    ]
    for load in loads:
        load.start()

    barrier = pltpu.get_barrier_semaphore()
    pl.semaphore_signal(barrier, inc=1, device_id=(dp, sibling), device_id_type=MESH)

    @pl.loop(1, n_y)
    def _(k):
        pl.semaphore_signal(barrier, inc=1, device_id=y_peer(k), device_id_type=MESH)

    @pl.loop(1, n_z)
    def _(k):
        pl.semaphore_signal(barrier, inc=1, device_id=z_peer(k), device_id_type=MESH)

    @pl.loop(1, n_x)
    def _(k):
        peer = lax.rem(x + k, n_x) * z_low + low_z
        pl.semaphore_signal(barrier, inc=1, device_id=(peer, me), device_id_type=MESH)

    def copy_small(source, target, slot, device):
        pltpu.make_async_remote_copy(
            src_ref=source,
            dst_ref=target,
            send_sem=small_send.at[slot],
            recv_sem=small_recv.at[slot],
            device_id=device,
            device_id_type=MESH,
        ).start()

    def wait_small(landing, count, slot, sems):
        part = landing.at[pl.ds(0, count)]
        pltpu.make_async_copy(part, part, sems.at[slot]).wait()

    def push_group(slot, source, landing):
        @pl.when(at_edge)
        def _():
            for there in served:

                @pl.loop(0, n_q)
                def _(k):
                    q = lax.rem(mine + k + n_q // 2, n_q)
                    peer = (q // 2) * 4 + (1 - half) * 2 + lax.rem(q, 2)
                    copy_small(source(q), landing.at[me], slot, (there, peer))

        @pl.loop(1, n_q)
        def _(k):
            move = n_q // 2 + (k // 2) * (1 - 2 * lax.rem(k, 2))
            q, device = column_peer(lax.rem(move, n_q))
            copy_small(source(q), landing.at[me], slot, device)

    def send_cen(slot, peer, part=slice(None), sem=None, there=dp, sent_sem=0):
        pltpu.make_async_remote_copy(
            src_ref=centres_hbm if slot is me else cen.at[slot, part],
            dst_ref=cen.at[slot, part],
            send_sem=cen_send.at[sent_sem],
            recv_sem=cen_recv.at[slot if sem is None else sem],
            device_id=(there, peer),
            device_id_type=MESH,
        ).start()

    def wait_cen(slot, part=slice(None), sem=None):
        landed = cen.at[slot, part]
        pltpu.make_async_copy(
            landed, landed, cen_recv.at[slot if sem is None else sem]
        ).wait()

    loads[0].wait()
    loads[1].wait()
    a_buf[me, :, 0:rows] = dir_ref[...]
    a_buf[me, :, rows : 2 * rows] = res_ref[...]
    pl.semaphore_wait(barrier, n_y + n_z + n_x - 2)

    @pl.when(at_edge)
    def _():
        for there in served:
            copy_small(a_buf.at[me], a_buf.at[me], 1, (there, across))

    @pl.loop(1, n_y)
    def _(k):
        copy_small(a_buf.at[me], a_buf.at[me], 0, y_peer(k))

    @pl.when(at_edge)
    def _():
        for there in served:
            send_cen(me, across, there=there, sent_sem=1)

    send_cen(me, up)
    send_cen(me, down)
    send_cen(me, sibling)

    @pl.loop(1, n_z)
    def _(k):
        pl.semaphore_signal(token, inc=1, device_id=z_peer(k), device_id_type=MESH)

    log2e = math.log2(math.e)
    unit = sharpness / depth * log2e
    loads[3].wait()
    for part in range(width // rows):
        block = smp[part * rows : (part + 1) * rows, :].astype(F32)
        square = block * block
        folded = square[:, 0:rows]
        for other in range(1, depth // rows):
            folded = folded + square[:, other * rows : (other + 1) * rows]
        norms = jnp.sum(folded.T, axis=0, keepdims=True)
        row_term[:, part * rows : (part + 1) * rows] = (2.0 * sharpness * log2e) - unit * norms
    loads[2].wait()

    def make_tile(slot):
        tile = slot // 2
        block = cen[pl.ds(2 * tile, 2)].reshape(2 * rows, depth)
        wide = block.astype(F32)
        norms = jnp.sum(wide * wide, axis=1, keepdims=True) * unit
        cross = lax.dot_general(
            block, smp[...], (((1,), (1,)), ((), ())), preferred_element_type=F32
        )
        power = cross * (2.0 * unit) + (row_term[...] - norms)
        tiles[tile] = jnp.exp2(power).astype(BF16)

    def twin(slot):
        return slot + 1 - 2 * core

    top, bottom = slice(0, rows // 2), slice(rows // 2, rows)
    up_two = lax.rem(me + 8, n_ce)
    down_two = lax.rem(me + n_ce - 8, n_ce)

    def ends(first, s):
        return lax.rem(first + n_ce - 4 * s, n_ce), lax.rem(first + 4 * s, n_ce)

    def pull_own(s):
        low, high = ends(me, s)
        wait_cen(low)
        if s < n_y // 2 - 1:
            send_cen(low, up)
        else:
            send_cen(low, up, top)
        send_cen(low, sibling)
        wait_cen(high)
        if s < n_y // 2 - 1:
            send_cen(high, down)
        else:
            send_cen(high, down, bottom, n_ce)
        send_cen(high, sibling)
        return [low, high]

    def pull_across(s):
        low, high = ends(across, s)
        wait_cen(low)
        if s == 2:
            send_cen(low, up_two, top)
            send_cen(low, up)
        send_cen(low, sibling)
        wait_cen(high)
        if s == 2:
            send_cen(high, down_two, bottom, n_ce + 1)
            send_cen(high, down)
        send_cen(high, sibling)
        return [low, high]

    def pull_far(first, sem):
        far = lax.rem(first + n_ce // 2, n_ce)
        wait_cen(far, top)
        wait_cen(far, bottom, sem)
        send_cen(far, sibling)
        return [far]

    def work(slots):
        for slot in slots:
            wait_cen(twin(slot))
            make_tile(slot)

    work([me])
    wait_small(a_buf, 1, 1, small_recv)

    @pl.loop(1, n_y)
    def _(k):
        copy_small(a_buf.at[across], a_buf.at[across], 2, y_peer(k))

    wait_cen(across)
    send_cen(across, up_two)
    send_cen(across, down_two)
    send_cen(across, up)
    send_cen(across, down)
    send_cen(across, sibling)
    near = pull_own(1)
    work([across] + near)
    wait_small(a_buf, n_y - 1, 0, small_recv)
    wait_small(a_buf, n_y - 1, 2, small_recv)

    @pl.loop(0, n_q)
    def _(k):
        copy_small(a_buf.at[2 * k + core], a_buf.at[2 * k + core], 8, (dp, sibling))

    next_own = pull_own(2)
    next_far = pull_across(2)

    wait_small(a_buf, n_q, 8, small_recv)
    loads[4].wait()
    acc = fac[:, 0:rows] * a_buf[0, :, 0:rows]
    for b in range(1, n_ce):
        acc = acc + fac[:, b * rows : (b + 1) * rows] * a_buf[b, :, 0:rows]
    m_buf[me] = jnp.sum(acc.T, axis=0, keepdims=True)
    push_group(3, lambda q: m_buf.at[me], m_buf)

    last_far = pull_across(1)
    work(next_own)
    farther = pull_own(3)
    work(next_far + last_far)
    last_own = pull_across(3)
    work(farther)
    far_across = pull_far(across, n_ce + 1)
    far_own = pull_far(me, n_ce)
    work(last_own + far_across)

    wait_small(m_buf, n_ce - 1, 3, small_recv)

    def weigh(slots, start=False):
        total = jnp.zeros_like(w_acc) if start else w_acc[...]
        for slot in slots:
            tile = slot // 2
            coeffs = jnp.concatenate([m_buf[2 * tile], m_buf[2 * tile + 1]], axis=1)
            coeffs = jnp.broadcast_to(coeffs, (16, 2 * rows)).astype(BF16)
            total = total + jnp.dot(coeffs, tiles[tile], preferred_element_type=F32)
        w_acc[...] = total

    weigh([me, across] + near + next_own + next_far, True)
    weigh(last_far + farther + last_own)
    work(far_own)
    weigh(far_across + far_own)
    weights = w_acc[...]
    upright = jnp.broadcast_to(weights[0:1], (rows, width)).T.astype(BF16)
    diagonal = lax.broadcasted_iota(jnp.int32, (rows, rows), 0) == lax.broadcasted_iota(
        jnp.int32, (rows, rows), 1
    )

    across_row = weights[0:1].astype(BF16).astype(F32)

    def far_first(k):
        return lax.rem(y + n_y // 2 + (k + 1) // 2 * (1 - 2 * lax.rem(k, 2)), n_y)

    @pl.loop(0, n_y)
    def _(k):
        row = far_first(k)
        part = jnp.dot(tiles[2 * row], upright, preferred_element_type=F32)
        for c in range(2):
            picked = jnp.where(diagonal, part[c * rows : (c + 1) * rows], 0.0)
            c_out[2 * row + c, :, 0:rows] = jnp.sum(picked, axis=0, keepdims=True)
            block = tiles[2 * row + 1, c * rows : (c + 1) * rows, :]
            acc = block[:, 0:rows].astype(F32) * across_row[:, 0:rows]
            for p in range(1, width // rows):
                cut = slice(p * rows, (p + 1) * rows)
                acc = acc + block[:, cut].astype(F32) * across_row[:, cut]
            c_out[2 * row + c, :, rows : 2 * rows] = jnp.sum(acc.T, axis=0, keepdims=True)
        there = row * 4 + half * 2
        copy_small(c_out.at[2 * row + 1 - core], c_buf.at[mine], 4, (dp, there + 1 - core))

        @pl.when(row != y)
        def _():
            copy_small(c_out.at[2 * row + core], c_buf.at[mine], 4, (dp, there + core))

    c_buf[mine] = c_out[mine]
    wait_small(c_buf, n_q - 1, 4, small_recv)
    both = jnp.sum(c_buf[...], axis=0)
    g_out[0] = both[:, 0:rows]
    g_out[1] = both[:, rows : 2 * rows]
    pl.semaphore_wait(token, n_z - 1)

    @pl.loop(0, n_p - 1)
    def _(k):
        side, device = plane_peer(k)
        copy_small(g_out.at[side], g_buf.at[place], 5, device)

    g_buf[place] = g_out[half]
    wait_small(g_buf, n_p - 1, 5, small_recv)
    columns = jnp.sum(g_buf[...], axis=0) * scale

    spread = jnp.broadcast_to(columns, (rows, rows)).T
    bend = m_buf[me] * columns
    @pl.loop(0, n_y)
    def _(k):
        row = far_first(k)
        for b in range(4):
            start = pl.multiple_of((4 * row + b) * rows, rows)
            i_out[row, :, b * rows : (b + 1) * rows] = jnp.sum(
                fac[:, pl.ds(start, rows)] * spread, axis=0, keepdims=True
            )
        i_out[row, :, 4 * rows : 5 * rows] = bend

        @pl.when(at_edge)
        def _():
            for there in served:
                for c in range(2):
                    peer = row * 4 + (1 - half) * 2 + c
                    copy_small(i_out.at[row], i_buf.at[me], 6, (there, peer))

        near_by = row * 4 + half * 2
        copy_small(i_out.at[row], i_buf.at[me], 6, (dp, near_by + 1 - core))

        @pl.when(row != y)
        def _():
            copy_small(i_out.at[row], i_buf.at[me], 6, (dp, near_by + core))

    i_buf[me] = i_out[y]
    whole_dir = a_buf[:, :, 0:rows]
    whole_res = a_buf[:, :, rows : 2 * rows]
    dir_norm = jnp.sum(jnp.sum(whole_dir * whole_dir, axis=0), axis=1, keepdims=True)
    old_norm = jnp.sum(jnp.sum(whole_res * whole_res, axis=0), axis=1, keepdims=True)
    wait_small(i_buf, n_ce - 1, 6, small_recv)
    summed = jnp.sum(i_buf[...], axis=0)
    curvature = jnp.sum(summed[:, 4 * rows :], axis=1, keepdims=True) + ridge * dir_norm
    alpha = old_norm / curvature
    squares = jnp.zeros((1, rows), F32)
    for b in range(4):
        own_dir = a_buf[4 * y + b, :, 0:rows]
        image = summed[:, b * rows : (b + 1) * rows] + ridge * own_dir
        left = a_buf[4 * y + b, :, rows : 2 * rows] - alpha * image
        squares = squares + left * left
        left_ref[b] = left
    e_buf[y] = squares

    @pl.loop(1, n_y)
    def _(k):
        peer = lax.rem(me + 4 * k, n_ce)
        copy_small(e_buf.at[y], e_buf.at[y], 7, (dp, peer))

    out_ref[0:1, :] = jnp.broadcast_to(alpha, (1, rows))
    out_ref[1:2, :] = left_ref[me - 4 * y]
    wait_small(e_buf, n_y - 1, 7, small_recv)
    new_norm = jnp.sum(jnp.sum(e_buf[...], axis=0), axis=1, keepdims=True)
    out_ref[2:3, :] = jnp.broadcast_to(new_norm / old_norm, (1, rows))

    for slot, landing, count in (
        (0, a_buf, n_y - 1),
        (2, a_buf, n_y - 1),
        (8, a_buf, n_q),
        (3, m_buf, n_q - 1),
        (4, c_buf, n_q - 1),
        (5, g_buf, n_p - 1),
        (6, i_buf, n_q - 1),
        (7, e_buf, n_y - 1),
    ):
        wait_small(landing, count, slot, small_send)

    @pl.when(at_edge)
    def _():
        wait_small(a_buf, 2, 1, small_send)
        wait_small(m_buf, n_ce, 3, small_send)
        wait_small(i_buf, n_ce, 6, small_send)
        crossed = cen.at[pl.ds(0, 2)]
        pltpu.make_async_copy(crossed, crossed, cen_send.at[1]).wait()

    sent = cen.at[pl.ds(0, n_ce - 2)]
    pltpu.make_async_copy(sent, sent, cen_send.at[0]).wait()


def on_device(n_dp, n_ce, samples, centres, factor, solution, residual, direction):
    rows, depth = centres.shape
    width = samples.shape[0]
    total_samples = width * n_dp * n_ce
    scale = 1.0 / (balance * total_samples * math.sqrt(rows * n_ce))
    hbm = pl.BlockSpec(memory_space=pltpu.HBM)
    n_q = n_ce // 2
    n_p = 2 * n_dp
    out = pl.pallas_call(
        functools.partial(step_kernel, n_dp, n_ce, scale),
        out_shape=jax.ShapeDtypeStruct((8, rows), F32),
        in_specs=[hbm] * 5,
        out_specs=pl.BlockSpec(memory_space=pltpu.VMEM),
        scratch_shapes=[
            pltpu.VMEM((width, depth), BF16),
            pltpu.VMEM((n_ce, rows, depth), BF16),
            pltpu.VMEM((rows, rows * n_ce), F32),
            pltpu.VMEM((1, rows), F32),
            pltpu.VMEM((1, rows), F32),
            pltpu.VMEM((n_ce // 2, 2 * rows, width), BF16),
            pltpu.VMEM((1, width), F32),
            pltpu.VMEM((n_ce, 1, 2 * rows), F32),
            pltpu.VMEM((n_ce, 1, rows), F32),
            pltpu.VMEM((n_q, 1, 2 * rows), F32),
            pltpu.VMEM((n_q, 1, 2 * rows), F32),
            pltpu.VMEM((2, 1, rows), F32),
            pltpu.VMEM((n_p, 1, rows), F32),
            pltpu.VMEM((n_ce // 4, 1, 5 * rows), F32),
            pltpu.VMEM((n_ce, 1, 5 * rows), F32),
            pltpu.VMEM((n_ce // 4, 1, rows), F32),
            pltpu.VMEM((4, 1, rows), F32),
            pltpu.VMEM((16, width), F32),
            pltpu.SemaphoreType.DMA((5,)),
            pltpu.SemaphoreType.DMA((n_ce + 2,)),
            pltpu.SemaphoreType.DMA((2,)),
            pltpu.SemaphoreType.DMA((9,)),
            pltpu.SemaphoreType.DMA((9,)),
            pltpu.SemaphoreType.REGULAR,
        ],
        compiler_params=pltpu.CompilerParams(
            collective_id=0, has_side_effects=True, vmem_limit_bytes=63 * 1024 * 1024
        ),
        cost_estimate=pl.CostEstimate(
            flops=2 * width * rows * n_ce * (depth + 2),
            bytes_accessed=4 * rows * rows * n_ce,
            transcendentals=width * rows * n_ce,
        ),
    )(samples, centres, factor, residual.reshape(1, rows), direction.reshape(1, rows))
    alpha, new_residual, ratio = out[0], out[1], out[2]
    return (solution + alpha * direction, new_residual, new_residual + ratio * direction)


def solution(mesh):
    return jax.shard_map(
        functools.partial(on_device, mesh.shape["dp"], mesh.shape["centre"]),
        mesh=mesh,
        in_specs=(
            P(("dp", "centre"), None),
            P("centre", None),
            P("centre", None),
            P("centre"),
            P("centre"),
            P("centre"),
        ),
        out_specs=(P("centre"), P("centre"), P("centre")),
        check_vma=False,
    )
```
